256 devices in a mesh: dp: 16 (over y, z_lo, core), ctx: 16 (over x, z_hi).
Axes of the slice: x: 4, y: 4, z: 8 (z_hi: 4, z_lo: 2; z = z_hi * 2 + z_lo), core: 2. Of those that a mesh axis runs over, the one named last changes fastest.
Arguments:
- text: bfloat16 [16, 2, 128, 2048], P('dp', None, None, 'ctx'), may hold values from -6 to 6
- src: int32 [16], replicated, may hold values from 0 to 15, each once
- lengths: int32 [16, 2], replicated, may hold values from 1 to 128
- kv_weight: bfloat16 [2048, 2, 8192], P('dp', None, 'ctx'), may hold values from -0.125 to 0.125
- queries: bfloat16 [16, 4096, 4096], P('dp', 'ctx'), may hold values from -160 to 160
- grad_out: bfloat16 [16, 4096, 4096], P('dp', 'ctx'), may hold values from -6 to 6
Outputs:
- attended: bfloat16 [16, 4096, 4096], P('dp', 'ctx')
- grad_queries: bfloat16 [16, 4096, 4096], P('dp', 'ctx')
- grad_weight: float32 [2048, 2, 8192], P('dp', None, 'ctx')
The draws below stay inside these ranges and needn't reach their ends.
Inputs may be any that keep to these rules, and one draw needn't show every extreme that they name: `src`: each text sample is used by exactly one latent sample. `lengths`: tokens of an encoder output at or beyond its length are padding.
All inputs are finite; a program needn't handle non-finite values.
Results may differ from the reference program's by a relative error of at most 0.018.
The reference program's roundings to bfloat16 on the way count: a program that leaves them out, or rounds other values in their place, can miss the bound.
Values may be sent and summed in bfloat16 or wider, within the bound.
No kernel may reach another device: no remote copies, remote signals or barrier semaphores. Data moves between devices by JAX's collectives and lax.ppermute only.
A program may use at most 128 MiB of HBM per device.

```python
import math
import jax
import jax.numpy as jnp
from jax import lax

HEAD = 128
E = 2048
TT = 128
HD = 4096
SAMPLES = 16
LAT = 4096


def draw_queries(key, part):
    base = jax.random.normal(jax.random.fold_in(key, 11), (SAMPLES, LAT, HD), jnp.float32)
    base = jnp.clip(base, -6.0, 6.0)
    return base.astype(jnp.bfloat16)


def set_ends(values, stream_key, smallest, largest):
    longest = values.shape.index(max(values.shape))
    spots = []
    for shift in (0, 1):
        where = [jax.random.randint(jax.random.fold_in(stream_key, axis), (), 0, length) for axis, length in enumerate(values.shape)]
        where[longest] = (where[longest] + shift) % values.shape[longest]
        spots.append(tuple(where))
    return values.at[spots[0]].set(smallest).at[spots[1]].set(largest)


def steps_of(stream_key, shape, split, smallest, top_value):
    def one(axis_at, blocks):
        heights = jax.random.uniform(jax.random.fold_in(jax.random.fold_in(stream_key, 6), axis_at), (blocks,), jnp.float32, smallest / len(split), top_value / len(split))
        return jnp.repeat(jnp.exp(heights), shape[axis_at] // blocks).reshape((-1,) + (1,) * (len(shape) - axis_at - 1))

    gain = one(*split[0])
    for cut in split[1:]:
        gain = gain * one(*cut)
    return gain


def noise(own_key, shape, scale, reach, pieces=(), kind=jnp.bfloat16):
    entries = scale * jax.random.normal(own_key, shape, jnp.float32)
    if pieces:
        entries = entries * steps_of(own_key, shape, pieces, -0.22, 0.18)
    return jnp.clip(entries, -reach, reach).astype(kind)


def setup_inputs(seed: int = 0) -> dict:
    streams_of = jax.random.split(jax.random.key(seed), 7)
    return {
        "text": noise(streams_of[0], (SAMPLES, 2, TT, E), 1.0, 6.0, ((0, 16), (3, 16))),
        "src": jax.random.permutation(streams_of[1], SAMPLES).astype(jnp.int32),
        "lengths": set_ends(jax.random.randint(streams_of[2], (SAMPLES, 2), 1, TT + 1), jax.random.fold_in(streams_of[2], 1), 1, TT).astype(jnp.int32),
        "kv_weight": noise(streams_of[3], (E, 2, 2 * HD), E ** -0.5, 0.125, ((0, 16), (2, 16))),
        "queries": draw_queries(jax.random.fold_in(streams_of[6], 71), 0),
        "grad_out": noise(streams_of[5], (SAMPLES, LAT, HD), 1.0, 6.0, ((0, 16), (1, 16))),
    }


def attend_one(query, key_value, valid, cotangent):
    length = query.shape[0]
    heads = query.shape[1] // HEAD
    keys = key_value.shape[0] * key_value.shape[1]
    scale = 1.0 / math.sqrt(HEAD)
    paired = key_value.reshape(keys, heads, 2, HEAD).astype(jnp.float32)
    key = paired[:, :, 0]
    value = paired[:, :, 1]
    q_rows = query.reshape(length, heads, HEAD).astype(jnp.float32)
    g_rows = cotangent.reshape(length, heads, HEAD).astype(jnp.float32)
    scores = jnp.einsum('lhd,jhd->hlj', q_rows, key) * scale
    scores = jnp.where(valid[None, None, :], scores, -1e+30)
    top = lax.optimization_barrier(jnp.max(scores, axis=-1, keepdims=True))
    weights = jnp.exp(scores - top)
    probs = weights / lax.optimization_barrier(jnp.sum(weights, axis=-1, keepdims=True))
    probs_low = lax.optimization_barrier(probs.astype(jnp.bfloat16)).astype(jnp.float32)
    attended = jnp.einsum('hlj,jhd->lhd', probs_low, value).reshape(length, heads * HEAD).astype(jnp.bfloat16)
    grad_probs = jnp.einsum('lhd,jhd->hlj', g_rows, value)
    delta = lax.optimization_barrier(jnp.sum(probs * grad_probs, axis=-1, keepdims=True))
    grad_scores = (probs * (grad_probs - delta) * scale).astype(jnp.bfloat16)
    grad_scores = lax.optimization_barrier(grad_scores).astype(jnp.float32)
    grad_queries = jnp.einsum('hlj,jhd->lhd', grad_scores, key).reshape(length, heads * HEAD).astype(jnp.bfloat16)
    grad_key = jnp.einsum('hlj,lhd->jhd', grad_scores, q_rows)
    grad_value = jnp.einsum('hlj,lhd->jhd', probs_low, g_rows)
    grad_kv = jnp.stack([grad_key, grad_value], axis=2).reshape(2, keys // 2, heads * 2 * HEAD)
    return (attended, grad_queries, grad_kv)

def reference(text, src, lengths, kv_weight, queries, grad_out):
    ctx_text = jnp.take(text, src.astype(jnp.int32), axis=0)
    wide_text = ctx_text.astype(jnp.float32)
    kv = jnp.einsum('betf,fec->betc', wide_text, kv_weight.astype(jnp.float32)).astype(jnp.bfloat16)
    chosen = jnp.take(lengths, src.astype(jnp.int32), axis=0)
    positions = jnp.arange(TT, dtype=jnp.int32)
    valid = (positions[None, None, :] < chosen[:, :, None]).reshape(SAMPLES, 2 * TT)

    def one_sample(items):
        return attend_one(items[0], items[1], items[2], items[3])
    attended, grad_queries, grad_kv = lax.map(one_sample, (queries, kv, valid, grad_out))
    grad_low = lax.optimization_barrier(grad_kv.astype(jnp.bfloat16)).astype(jnp.float32)
    grad_weight = jnp.einsum('betf,betc->fec', wide_text, grad_low)
    return (attended, grad_queries, grad_weight)
```

```python
import math

import jax
import jax.numpy as jnp
from jax import lax
from jax.experimental import pallas as pl
from jax.experimental.pallas import tpu as pltpu
from jax.sharding import PartitionSpec as P

HEAD = 128
N = 4
GROUPS = ((0, 1), (3, 2))
BF = jnp.bfloat16
F32 = jnp.float32


def x_shift(a, k):
    return lax.ppermute(
        a, "ctx", [(4 * x + z, 4 * ((x + k) % N) + z) for x in range(N) for z in range(N)]
    )


def z_shift(a, m):
    return lax.ppermute(
        a, "ctx", [(4 * x + z, 4 * x + (z + m) % N) for x in range(N) for z in range(N)]
    )


def dot(a, b, dims):
    return lax.dot_general(a, b, (dims, ((), ())), preferred_element_type=F32)


def pack(group, where, queries, grad_out):
    def body(s, q, g, *rest):
        outs, sem = rest[:-1], rest[-1]
        copies = []
        for k in (1, 2, 3):
            for a, src in enumerate((q, g)):
                for n, m in enumerate(group):
                    col = pl.multiple_of(
                        lax.rem(s[0] + k, N) * 1024 + lax.rem(s[1] + N - m, N) * 256, 256
                    )
                    copies.append(
                        pltpu.make_async_copy(
                            src.at[:, pl.ds(col, 256)],
                            outs[k - 1].at[a, n],
                            sem.at[len(copies)],
                        )
                    )
        for c in copies:
            c.start()
        for c in copies:
            c.wait()

    return pl.pallas_call(
        body,
        grid_spec=pltpu.PrefetchScalarGridSpec(
            num_scalar_prefetch=1,
            grid=(1,),
            in_specs=[pl.BlockSpec(memory_space=pl.ANY)] * 2,
            out_specs=[pl.BlockSpec(memory_space=pl.ANY)] * 3,
            scratch_shapes=[pltpu.SemaphoreType.DMA((6 * len(group),))],
        ),
        out_shape=[jax.ShapeDtypeStruct((2, len(group), 256, 256), BF)] * 3,
        name="pack",
    )(where, queries, grad_out)


def project(where, pieces, weight):
    def block(n, k, s):
        return lax.rem(s[0] + N - k, N) * N + lax.rem(s[1] + N - n, N)

    def body(s, t0, t1, t2, t3, w, kv, ordered, acc):
        n, k = pl.program_id(0), pl.program_id(1)

        @pl.when((n == 0) & (k == 0))
        def _():
            acc[...] = jnp.zeros_like(acc)

        for i, t in enumerate((t0, t1, t2, t3)):

            @pl.when(n == i)
            def _(t=t):
                ordered[...] = t[...]
                for e in range(2):
                    acc[e] += dot(t[0, e], w[0, e], ((1,), (0,)))

        @pl.when((n == N - 1) & (k == N - 1))
        def _():
            kv[...] = acc[...].astype(BF)

    return pl.pallas_call(
        body,
        grid_spec=pltpu.PrefetchScalarGridSpec(
            num_scalar_prefetch=1,
            grid=(N, N),
            in_specs=[pl.BlockSpec((1, 2, 128, 128), lambda n, k, s: (k, 0, 0, 0))] * 4
            + [pl.BlockSpec((1, 2, 128, 512), lambda n, k, s: (block(n, k, s), 0, 0, 0))],
            out_specs=[
                pl.BlockSpec((2, 128, 512), lambda n, k, s: (0, 0, 0)),
                pl.BlockSpec((1, 2, 128, 128), lambda n, k, s: (block(n, k, s), 0, 0, 0)),
            ],
            scratch_shapes=[pltpu.VMEM((2, 128, 512), F32)],
        ),
        out_shape=[
            jax.ShapeDtypeStruct((2, 128, 512), BF),
            jax.ShapeDtypeStruct((16, 2, 128, 128), BF),
        ],
        cost_estimate=pl.CostEstimate(
            flops=2 * 256 * 2048 * 512, bytes_accessed=6 << 20, transcendentals=0
        ),
        name="project",
    )(where, *pieces, weight)


def attend(group, where, queries, grad_out, moved, kvs):
    count = len(group)
    scale = 1.0 / math.sqrt(HEAD)

    def body(s, *refs):
        own_q, own_g = refs[:count], refs[count : 2 * count]
        sent = refs[2 * count : 2 * count + 3]
        kv = refs[2 * count + 3 : 3 * count + 3]
        outs = refs[3 * count + 3 : 3 * count + 7]
        grads = refs[3 * count + 7 :]
        row = lax.broadcasted_iota(jnp.int32, (256, 256), 0)
        valid = row < jnp.where(row < 128, s[2], s[3] + 128)
        for n in range(count):
            key, value = kv[n][:, :HEAD], kv[n][:, HEAD:]
            grad_key = grad_value = None
            for k in range(N):
                if k == 0:
                    q, g = own_q[n][...], own_g[n][...]
                else:
                    q, g = sent[k - 1][0, n], sent[k - 1][1, n]
                scores = dot(key, q, ((1,), (1,))) * scale
                scores = jnp.where(valid, scores, -1e30)
                weights = jnp.exp(scores - jnp.max(scores, axis=0, keepdims=True))
                probs = weights * (1.0 / jnp.sum(weights, axis=0, keepdims=True))
                low = probs.astype(BF)
                outs[k][0, n] = dot(low, value, ((0,), (0,))).astype(BF)
                grad_probs = dot(value, g, ((1,), (1,)))
                delta = jnp.sum(probs * grad_probs, axis=0, keepdims=True)
                grad_scores = (probs * (grad_probs - delta) * scale).astype(BF)
                outs[k][1, n] = dot(grad_scores, key, ((0,), (0,))).astype(BF)
                dk = dot(grad_scores, q, ((1,), (0,)))
                dv = dot(low, g, ((1,), (0,)))
                grad_key = dk if k == 0 else grad_key + dk
                grad_value = dv if k == 0 else grad_value + dv
            grads[n][:, :HEAD] = grad_key.astype(grads[n].dtype)
            grads[n][:, HEAD:] = grad_value.astype(grads[n].dtype)

    def own(m):
        return pl.BlockSpec(
            (256, HEAD), lambda l, s: (0, s[0] * 8 + lax.rem(s[1] + N - m, N) * 2 + l)
        )

    by_head = pl.BlockSpec((2, count, 256, HEAD), lambda l, s: (0, 0, 0, l))
    return pl.pallas_call(
        body,
        grid_spec=pltpu.PrefetchScalarGridSpec(
            num_scalar_prefetch=1,
            grid=(2,),
            in_specs=[own(m) for m in group] * 2
            + [by_head] * 3
            + [pl.BlockSpec((256, 256), lambda l, s: (0, l))] * count,
            out_specs=[by_head] * 4 + [pl.BlockSpec((256, 256), lambda l, s: (0, l))] * count,
        ),
        out_shape=[jax.ShapeDtypeStruct((2, count, 256, 256), BF)] * 4
        + [jax.ShapeDtypeStruct((256, 512), BF if m else F32) for m in group],
        cost_estimate=pl.CostEstimate(
            flops=12 * count * 2 * 1024 * 256 * 128,
            bytes_accessed=count * (4 << 20),
            transcendentals=count * 2 * 1024 * 256,
        ),
        compiler_params=pltpu.CompilerParams(vmem_limit_bytes=48 << 20),
        name="attend",
    )(where, *([queries] * count), *([grad_out] * count), *moved, *kvs)


def place(group, where, pieces, before):
    def body(s, p0, p1, p2, p3, *rest):
        outs, sem = rest[-3:-1], rest[-1]
        copies = []
        for k, p in enumerate((p0, p1, p2, p3)):
            for a in range(2):
                for n, m in enumerate(group):
                    col = pl.multiple_of(
                        lax.rem(s[0] + k, N) * 1024 + lax.rem(s[1] + N - m, N) * 256, 256
                    )
                    copies.append(
                        pltpu.make_async_copy(
                            p.at[a, n], outs[a].at[:, pl.ds(col, 256)], sem.at[len(copies)]
                        )
                    )
        for c in copies:
            c.start()
        for c in copies:
            c.wait()

    extra = [] if before is None else list(before)
    return pl.pallas_call(
        body,
        grid_spec=pltpu.PrefetchScalarGridSpec(
            num_scalar_prefetch=1,
            grid=(1,),
            in_specs=[pl.BlockSpec(memory_space=pl.ANY)] * (4 + len(extra)),
            out_specs=[pl.BlockSpec(memory_space=pl.ANY)] * 2,
            scratch_shapes=[pltpu.SemaphoreType.DMA((8 * len(group),))],
        ),
        out_shape=[jax.ShapeDtypeStruct((256, 4096), BF)] * 2,
        input_output_aliases={5: 0, 6: 1} if extra else {},
        name="place",
    )(where, *pieces, *extra)


def per_device(text, src, lengths, kv_weight, queries, grad_out):
    group = lax.axis_index("dp")
    ctx = lax.axis_index("ctx")
    sample = lax.dynamic_index_in_dim(src, group, 0, keepdims=False)
    limits = lax.dynamic_index_in_dim(lengths, sample, 0, keepdims=False)
    where = jnp.stack([ctx // N, ctx % N, limits[0], limits[1]]).astype(jnp.int32)
    q, g = queries[0], grad_out[0]

    everyone = lax.all_gather(text[0], "dp", axis=0)
    weight = lax.all_gather(jnp.swapaxes(kv_weight, 0, 1), "dp", axis=0)
    picked = lax.dynamic_index_in_dim(everyone, sample, 0, keepdims=False)
    along_x = jnp.stack([picked] + [x_shift(picked, k) for k in (1, 2, 3)])
    pieces = [along_x] + [z_shift(along_x, n) for n in (1, 2, 3)]

    moved = {}
    for ms in GROUPS:
        sends = pack(ms, where, q, g)
        moved[ms] = [x_shift(a, k + 1) for k, a in enumerate(sends)]

    kv, ordered = project(where, pieces, weight)
    kv = kv.reshape(256, 512)
    kvs = [kv] + [z_shift(kv, m) for m in (1, 2, 3)]
    own_rows = lax.all_to_all(ordered, "dp", split_axis=0, concat_axis=0, tiled=True)

    grads = [None] * N
    out = None
    for ms in GROUPS:
        res = attend(ms, where, q, g, moved[ms], [kvs[m] for m in ms])
        back = [res[0]] + [x_shift(res[k], N - k) for k in (1, 2, 3)]
        for m, d in zip(ms, res[4:]):
            grads[m] = d if m == 0 else z_shift(d, N - m)
        out = place(ms, where, back, out)

    total = grads[0] + sum(grads[m].astype(F32) for m in (1, 2, 3))
    every_grad = lax.all_gather(total.astype(BF).reshape(2, 128, 512), "dp", axis=0)
    grad_weight = jnp.einsum(
        "betf,betc->fec", own_rows, every_grad, preferred_element_type=F32
    )
    return (out[0][None], out[1][None], grad_weight)


def solution(mesh):
    placed = (
        P("dp", None, None, "ctx"),
        P(),
        P(),
        P("dp", None, "ctx"),
        P("dp", "ctx", None),
        P("dp", "ctx", None),
    )
    return jax.shard_map(
        per_device,
        mesh=mesh,
        in_specs=placed,
        out_specs=(P("dp", "ctx", None), P("dp", "ctx", None), P("dp", None, "ctx")),
        check_vma=False,
    )
```

```python
import math

import jax
import jax.numpy as jnp
from jax import lax
from jax.experimental import pallas as pl
from jax.experimental.pallas import tpu as pltpu
from jax.sharding import PartitionSpec as P

HEAD = 128
N = 4
GROUPS = ((0, 1), (3, 2))
BF = jnp.bfloat16
F32 = jnp.float32


def x_shift(a, k):
    return lax.ppermute(
        a, "ctx", [(4 * x + z, 4 * ((x + k) % N) + z) for x in range(N) for z in range(N)]
    )


def z_shift(a, m):
    return lax.ppermute(
        a, "ctx", [(4 * x + z, 4 * x + (z + m) % N) for x in range(N) for z in range(N)]
    )


def dot(a, b, dims):
    return lax.dot_general(a, b, (dims, ((), ())), preferred_element_type=F32)


def pack(group, where, queries, grad_out):
    count = len(group)

    def body(s, *refs):
        ins, outs = refs[: 6 * count], refs[6 * count :]
        for k in range(3):
            for n in range(count):
                for a in range(2):
                    outs[k][a, n] = ins[(k * count + n) * 2 + a][...]

    def columns(k, m):
        return pl.BlockSpec(
            (256, 256), lambda i, s: (0, lax.rem(s[0] + k, N) * 4 + lax.rem(s[1] + N - m, N))
        )

    whole = pl.BlockSpec((2, count, 256, 256), lambda i, s: (0, 0, 0, 0))
    return pl.pallas_call(
        body,
        grid_spec=pltpu.PrefetchScalarGridSpec(
            num_scalar_prefetch=1,
            grid=(1,),
            in_specs=[columns(k, m) for k in (1, 2, 3) for m in group for _ in range(2)],
            out_specs=[whole] * 3,
        ),
        out_shape=[jax.ShapeDtypeStruct((2, count, 256, 256), BF)] * 3,
        cost_estimate=pl.CostEstimate(
            flops=0, bytes_accessed=count * (3 << 20) // 2, transcendentals=0
        ),
        compiler_params=pltpu.CompilerParams(vmem_limit_bytes=32 << 20),
        name="pack",
    )(where, *([queries, grad_out] * (3 * count)))


def project(where, pieces, weight):
    def body(s, t0, t1, t2, t3, w, kv, ordered, acc):
        n = pl.program_id(0)
        for i, t in enumerate((t0, t1, t2, t3)):

            @pl.when(n == i)
            def _(t=t, i=i):
                for e in range(2):
                    part = None
                    for k in range(N):
                        at = lax.rem(s[0] + N - k, N)
                        d = dot(t[k, e], w[at, 0, e], ((1,), (0,)))
                        part = d if part is None else part + d
                    if i == 0:
                        acc[e] = part
                    elif i < N - 1:
                        acc[e] += part
                    else:
                        kv[e] = (acc[e] + part).astype(BF)
                for k in range(N):
                    ordered[lax.rem(s[0] + N - k, N), 0] = t[k]

    whole = pl.BlockSpec((N, 2, 128, 128), lambda n, s: (0, 0, 0, 0))
    return pl.pallas_call(
        body,
        grid_spec=pltpu.PrefetchScalarGridSpec(
            num_scalar_prefetch=1,
            grid=(N,),
            in_specs=[whole] * 4
            + [
                pl.BlockSpec(
                    (N, 1, 2, 128, 512), lambda n, s: (0, lax.rem(s[1] + N - n, N), 0, 0, 0)
                )
            ],
            out_specs=[
                pl.BlockSpec((2, 128, 512), lambda n, s: (0, 0, 0)),
                pl.BlockSpec(
                    (N, 1, 2, 128, 128), lambda n, s: (0, lax.rem(s[1] + N - n, N), 0, 0, 0)
                ),
            ],
            scratch_shapes=[pltpu.VMEM((2, 128, 512), F32)],
        ),
        out_shape=[
            jax.ShapeDtypeStruct((2, 128, 512), BF),
            jax.ShapeDtypeStruct((N, N, 2, 128, 128), BF),
        ],
        cost_estimate=pl.CostEstimate(
            flops=2 * 256 * 2048 * 512, bytes_accessed=6 << 20, transcendentals=0
        ),
        compiler_params=pltpu.CompilerParams(vmem_limit_bytes=32 << 20),
        name="project",
    )(where, *pieces, weight.reshape(N, N, 2, 128, 512))


def weight_gradient(where, pieces, grads):
    def body(s, t0, t1, t2, t3, d, out):
        n = pl.program_id(0)
        for i, t in enumerate((t0, t1, t2, t3)):

            @pl.when(n == i)
            def _(t=t, i=i):
                for e in range(2):
                    part = None
                    for k in range(N):
                        at = lax.rem(s[4] + N - k, N)
                        p = dot(t[k, e], d[at, 0, e], ((0,), (0,)))
                        part = p if part is None else part + p
                    if i == 0:
                        out[e] = part
                    else:
                        out[e] += part

    whole = pl.BlockSpec((N, 2, 128, 128), lambda n, s: (0, 0, 0, 0))
    return pl.pallas_call(
        body,
        grid_spec=pltpu.PrefetchScalarGridSpec(
            num_scalar_prefetch=1,
            grid=(N,),
            in_specs=[whole] * 4
            + [
                pl.BlockSpec(
                    (N, 1, 2, 128, 512), lambda n, s: (0, lax.rem(s[5] + n, N), 0, 0, 0)
                )
            ],
            out_specs=pl.BlockSpec((2, 128, 512), lambda n, s: (0, 0, 0)),
        ),
        out_shape=jax.ShapeDtypeStruct((2, 128, 512), F32),
        cost_estimate=pl.CostEstimate(
            flops=2 * 256 * 2048 * 512, bytes_accessed=6 << 20, transcendentals=0
        ),
        compiler_params=pltpu.CompilerParams(vmem_limit_bytes=32 << 20),
        name="weight_gradient",
    )(where, *pieces, grads.reshape(N, N, 2, 128, 512))


def own_text(where, ordered):
    y, r = where[4], where[5]

    def shift(a, step):
        return lax.ppermute(a, "dp", [(i, step(i)) for i in range(16)])

    def block(a, at):
        return lax.dynamic_index_in_dim(a, at, 0, keepdims=False)

    arrived = [block(ordered, y)]
    for k in (1, 2, 3):
        arrived.append(
            shift(block(ordered, (y + k) % N), lambda i, k=k: (i // N + k) % N * N + i % N)
        )
    by_r = jnp.stack(arrived, axis=1)
    pieces = [block(by_r, r)]
    for n in (1, 2, 3):
        pieces.append(
            shift(block(by_r, (r + N - n) % N), lambda i, n=n: i // N * N + (i % N - n) % N)
        )
    return pieces


def attend(group, where, queries, grad_out, moved, kvs):
    count = len(group)
    scale = 1.0 / math.sqrt(HEAD)

    def body(s, *refs):
        own_q, own_g = refs[:count], refs[count : 2 * count]
        sent = refs[2 * count : 2 * count + 3]
        kv = refs[2 * count + 3 : 3 * count + 3]
        outs = refs[3 * count + 3 : 3 * count + 7]
        grads = refs[3 * count + 7 :]
        row = lax.broadcasted_iota(jnp.int32, (256, 256), 0)
        valid = row < jnp.where(row < 128, s[2], s[3] + 128)
        for n in range(count):
            key, value = kv[n][:, :HEAD], kv[n][:, HEAD:]
            grad_key = grad_value = None
            for k in range(N):
                if k == 0:
                    q, g = own_q[n][...], own_g[n][...]
                else:
                    q, g = sent[k - 1][0, n], sent[k - 1][1, n]
                scores = dot(key, q, ((1,), (1,))) * scale
                scores = jnp.where(valid, scores, -1e30)
                weights = jnp.exp(scores - jnp.max(scores, axis=0, keepdims=True))
                probs = weights * (1.0 / jnp.sum(weights, axis=0, keepdims=True))
                low = probs.astype(BF)
                outs[k][0, n] = dot(low, value, ((0,), (0,))).astype(BF)
                grad_probs = dot(value, g, ((1,), (1,)))
                delta = jnp.sum(probs * grad_probs, axis=0, keepdims=True)
                grad_scores = (probs * (grad_probs - delta) * scale).astype(BF)
                outs[k][1, n] = dot(grad_scores, key, ((0,), (0,))).astype(BF)
                dk = dot(grad_scores, q, ((1,), (0,)))
                dv = dot(low, g, ((1,), (0,)))
                grad_key = dk if k == 0 else grad_key + dk
                grad_value = dv if k == 0 else grad_value + dv
            grads[n][:, :HEAD] = grad_key.astype(grads[n].dtype)
            grads[n][:, HEAD:] = grad_value.astype(grads[n].dtype)

    def own(m):
        return pl.BlockSpec(
            (256, HEAD), lambda l, s: (0, s[0] * 8 + lax.rem(s[1] + N - m, N) * 2 + l)
        )

    by_head = pl.BlockSpec((2, count, 256, HEAD), lambda l, s: (0, 0, 0, l))
    return pl.pallas_call(
        body,
        grid_spec=pltpu.PrefetchScalarGridSpec(
            num_scalar_prefetch=1,
            grid=(2,),
            in_specs=[own(m) for m in group] * 2
            + [by_head] * 3
            + [pl.BlockSpec((256, 256), lambda l, s: (0, l))] * count,
            out_specs=[by_head] * 4 + [pl.BlockSpec((256, 256), lambda l, s: (0, l))] * count,
        ),
        out_shape=[jax.ShapeDtypeStruct((2, count, 256, 256), BF)] * 4
        + [jax.ShapeDtypeStruct((256, 512), BF if m else F32) for m in group],
        cost_estimate=pl.CostEstimate(
            flops=12 * count * 2 * 1024 * 256 * 128,
            bytes_accessed=count * (4 << 20),
            transcendentals=count * 2 * 1024 * 256,
        ),
        compiler_params=pltpu.CompilerParams(vmem_limit_bytes=48 << 20),
        name="attend",
    )(where, *([queries] * count), *([grad_out] * count), *moved, *kvs)


def place(group, where, pieces, before):
    count = len(group)

    def body(s, p0, p1, p2, p3, *rest):
        outs = rest[-2:]
        for k, p in enumerate((p0, p1, p2, p3)):

            @pl.when(pl.program_id(1) == k)
            def _(p=p):
                for a in range(2):
                    outs[a][...] = p[a, 0]

    def column(n, k, s):
        m = group[0]
        for i in range(1, count):
            m = jnp.where(n == i, group[i], m)
        return (0, lax.rem(s[0] + k, N) * 4 + lax.rem(s[1] + N - m, N))

    extra = [] if before is None else list(before)
    return pl.pallas_call(
        body,
        grid_spec=pltpu.PrefetchScalarGridSpec(
            num_scalar_prefetch=1,
            grid=(count, N),
            in_specs=[pl.BlockSpec((2, 1, 256, 256), lambda n, k, s: (0, n, 0, 0))] * 4
            + [pl.BlockSpec(memory_space=pl.ANY)] * len(extra),
            out_specs=[pl.BlockSpec((256, 256), column)] * 2,
        ),
        out_shape=[jax.ShapeDtypeStruct((256, 4096), BF)] * 2,
        input_output_aliases={5: 0, 6: 1} if extra else {},
        cost_estimate=pl.CostEstimate(
            flops=0, bytes_accessed=count * (2 << 20), transcendentals=0
        ),
        name="place",
    )(where, *pieces, *extra)


def per_device(text, src, lengths, kv_weight, queries, grad_out):
    group = lax.axis_index("dp")
    ctx = lax.axis_index("ctx")
    sample = lax.dynamic_index_in_dim(src, group, 0, keepdims=False)
    limits = lax.dynamic_index_in_dim(lengths, sample, 0, keepdims=False)
    where = jnp.stack([ctx // N, ctx % N, limits[0], limits[1], group // N, group % N])
    where = where.astype(jnp.int32)
    q, g = queries[0], grad_out[0]

    everyone = lax.all_gather(text[0], "dp", axis=0)
    weight = lax.all_gather(jnp.swapaxes(kv_weight, 0, 1), "dp", axis=0)
    picked = lax.dynamic_index_in_dim(everyone, sample, 0, keepdims=False)
    along_x = jnp.stack([picked] + [x_shift(picked, k) for k in (1, 2, 3)])
    pieces = [along_x] + [z_shift(along_x, n) for n in (1, 2, 3)]

    moved = {}
    for ms in GROUPS:
        sends = pack(ms, where, q, g)
        moved[ms] = [x_shift(a, k + 1) for k, a in enumerate(sends)]

    kv, ordered = project(where, pieces, weight)
    kv = kv.reshape(256, 512)
    kvs = [kv] + [z_shift(kv, m) for m in (1, 2, 3)]
    own_rows = own_text(where, ordered)

    grads = [None] * N
    out = None
    for ms in GROUPS:
        res = attend(ms, where, q, g, moved[ms], [kvs[m] for m in ms])
        back = [res[0]] + [x_shift(res[k], N - k) for k in (1, 2, 3)]
        for m, d in zip(ms, res[4:]):
            grads[m] = d if m == 0 else z_shift(d, N - m)
        out = place(ms, where, back, out)

    total = grads[0] + sum(grads[m].astype(F32) for m in (1, 2, 3))
    every_grad = lax.all_gather(total.astype(BF).reshape(2, 128, 512), "dp", axis=0)
    grad_weight = jnp.swapaxes(weight_gradient(where, own_rows, every_grad), 0, 1)
    return (out[0][None], out[1][None], grad_weight)


def solution(mesh):
    placed = (
        P("dp", None, None, "ctx"),
        P(),
        P(),
        P("dp", None, "ctx"),
        P("dp", "ctx", None),
        P("dp", "ctx", None),
    )
    return jax.shard_map(
        per_device,
        mesh=mesh,
        in_specs=placed,
        out_specs=(P("dp", "ctx", None), P("dp", "ctx", None), P("dp", None, "ctx")),
        check_vma=False,
    )
```

```python
import math

import jax
import jax.numpy as jnp
from jax import lax
from jax.experimental import pallas as pl
from jax.experimental.pallas import tpu as pltpu
from jax.sharding import PartitionSpec as P

HEAD = 128
N = 4
ALONG_X = [[4 * x + z for x in range(N)] for z in range(N)]
BF = jnp.bfloat16
F32 = jnp.float32
PARAMS = pltpu.CompilerParams(vmem_limit_bytes=60 << 20)
ANY = pl.BlockSpec(memory_space=pl.ANY)
ORDER = (0, 1, 3, 2)
PARTS = ((0, 0, 1), (0, 1, 1), (1, 0, 1), (1, 1, 1))


def x_shift(a, k):
    return lax.ppermute(
        a, "ctx", [(4 * x + z, 4 * ((x + k) % N) + z) for x in range(N) for z in range(N)]
    )


def z_shift(a, m):
    return lax.ppermute(
        a, "ctx", [(4 * x + z, 4 * x + (z + m) % N) for x in range(N) for z in range(N)]
    )


def y_shift(a, k):
    return lax.ppermute(a, "dp", [(i, (i // N + k) % N * N + i % N) for i in range(16)])


def r_shift(a, n):
    return lax.ppermute(a, "dp", [(i, i // N * N + (i % N + n) % N) for i in range(16)])


def exchange_x(a):
    return lax.all_to_all(
        a, "ctx", split_axis=0, concat_axis=0, tiled=True, axis_index_groups=ALONG_X
    )


def dot(a, b, dims):
    return lax.dot_general(a, b, (dims, ((), ())), preferred_element_type=F32)


def minus(a, b):
    return lax.rem(a + N - b, N)


def whole(shape):
    return pl.BlockSpec(shape, lambda *_: (0,) * len(shape))


def call(body, scalars, grid, in_specs, out_specs, out_shape, name, cost, scratch=(), alias=()):
    return pl.pallas_call(
        body,
        grid_spec=pltpu.PrefetchScalarGridSpec(
            num_scalar_prefetch=len(scalars),
            grid=grid,
            in_specs=in_specs,
            out_specs=out_specs,
            scratch_shapes=list(scratch),
        ),
        out_shape=out_shape,
        input_output_aliases=dict(alias),
        cost_estimate=pl.CostEstimate(flops=cost[0], bytes_accessed=cost[1], transcendentals=0),
        compiler_params=PARAMS,
        name=name,
    )


def small(body, scalars, arrays, after, out_shape, name):
    here = pl.BlockSpec(memory_space=pltpu.VMEM)
    return pl.pallas_call(
        body,
        in_specs=[pl.BlockSpec(memory_space=pltpu.SMEM)] * len(scalars)
        + [here] * len(arrays) + [ANY] * len(after),
        out_specs=jax.tree.map(lambda _: here, out_shape),
        out_shape=out_shape,
        cost_estimate=pl.CostEstimate(flops=0, bytes_accessed=1 << 19, transcendentals=0),
        compiler_params=pltpu.CompilerParams(vmem_limit_bytes=16 << 20),
        name=name,
    )(*scalars, *arrays, *after)


def text_to_send(where, src, near):
    def body(w, src, *refs):
        for k in range(N):
            sample = src[lax.rem(w[2] + k, N) * N + w[3]]
            at = minus(lax.rem(sample, N), w[3])
            for n in range(N):

                @pl.when(at == n)
                def _(n=n, k=k):
                    refs[N + k][...] = refs[n][...]

    one = jax.ShapeDtypeStruct((2, 128, 128), BF)
    return small(body, (where, src), near, (), [one] * N, "text_to_send")


def text_that_came(where, src, came):
    def body(w, src, *refs):
        at = minus(w[2], src[w[2] * N + w[3]] // N)
        for k in range(N):

            @pl.when(at == k)
            def _(k=k):
                refs[N][...] = refs[k][...]

    one = jax.ShapeDtypeStruct((2, 128, 128), BF)
    return small(body, (where, src), came, (), one, "text_that_came")


def tiny(a):
    return a[(0,) * (a.ndim - 2)][:16, :128]


def pack(order, where, queries, grad_out, after):
    rows = 64

    def body(w, q, g, *rest):
        out = rest[-1]
        for x in range(N):
            for i, m in enumerate(order):
                col = pl.multiple_of((x * N + minus(w[1], m)) * 256, 256)
                out[x, 0, i] = q[:, pl.ds(col, 256)]
                out[x, 1, i] = g[:, pl.ds(col, 256)]

    return call(
        body, (where,), (256 // rows,),
        [pl.BlockSpec((rows, 4096), lambda i, w: (i, 0))] * 2 + [ANY] * len(after),
        pl.BlockSpec((N, 2, len(order), rows, 256), lambda i, w: (0, 0, 0, i, 0)),
        jax.ShapeDtypeStruct((N, 2, len(order), 256, 256), BF), "pack", (0, 6 << 20),
    )(where, queries, grad_out, *after)


def project(where, pieces, weight):
    def body(w, t0, t1, t2, t3, wt, kv, *rest):
        rows, acc = rest[:N], rest[N]
        k = pl.program_id(0)
        for i, t in enumerate((t0, t1, t2, t3)):

            @pl.when(k == i)
            def _(t=t, i=i):
                for e in range(2):
                    part = None
                    for n in range(N):
                        d = dot(t[n, e], wt[0, minus(w[1], n), e], ((1,), (0,)))
                        part = d if part is None else part + d
                    if i == 0:
                        acc[e] = part
                    elif i < N - 1:
                        acc[e] += part
                    else:
                        kv[e] = (acc[e] + part).astype(BF)
                for j in range(N):

                    @pl.when(minus(minus(w[0], i), w[2]) == j)
                    def _():
                        for n in range(N):
                            rows[j][minus(w[1], n)] = t[n]

    def at(k, w):
        return (minus(w[0], k), 0, 0, 0, 0)

    quarter = (N, 2, 128, 128)
    kv, *rows = call(
        body, (where,), (N,),
        [whole(quarter)] * N + [pl.BlockSpec((1, N, 2, 128, 512), at)],
        [whole((2, 128, 512))] + [whole(quarter)] * N,
        [jax.ShapeDtypeStruct((2, 128, 512), BF)] + [jax.ShapeDtypeStruct(quarter, BF)] * N,
        "project", (2 * 256 * 2048 * 512, 6 << 20), [pltpu.VMEM((2, 128, 512), F32)],
    )(where, *pieces, weight.reshape(N, N, 2, 128, 512))
    return kv.reshape(256, 512), rows


def attend(order, first, where, src, lengths, moved, kvs, into, wait):
    count = len(order)
    scale = 1.0 / math.sqrt(HEAD)

    def body(w, src, lengths, sent, *refs):
        kvs, kv, total = refs[:count], refs[-2], refs[-1]
        out, grads = refs[-3 - count], refs[-2 - count : -2]
        p = pl.program_id(0)
        cols = pl.ds(pl.multiple_of(pl.program_id(1) * 256, 256), 256)
        for i in range(count):

            @pl.when(p == i)
            def _(i=i):
                kv[...] = kvs[i][:, cols]

        sample = src[w[2] * N + w[3]]
        row = lax.broadcasted_iota(jnp.int32, (256, 256), 0)
        valid = row < jnp.where(row < 128, lengths[2 * sample], lengths[2 * sample + 1] + 128)
        key, value = kv[:, :HEAD], kv[:, HEAD:]
        grad_key = grad_value = None
        for x in range(N):
            q, g = sent[x, 0, 0], sent[x, 1, 0]
            scores = dot(key, q, ((1,), (1,))) * scale
            scores = jnp.where(valid, scores, -1e30)
            weights = jnp.exp(scores - jnp.max(scores, axis=0, keepdims=True))
            probs = weights * (1.0 / jnp.sum(weights, axis=0, keepdims=True))
            low = probs.astype(BF)
            out[x, 0, 0] = dot(low, value, ((0,), (0,))).astype(BF)
            grad_probs = dot(value, g, ((1,), (1,)))
            delta = jnp.sum(probs * grad_probs, axis=0, keepdims=True)
            grad_scores = (probs * (grad_probs - delta) * scale).astype(BF)
            out[x, 1, 0] = dot(grad_scores, key, ((0,), (0,))).astype(BF)
            dk = dot(grad_scores, q, ((1,), (0,)))
            dv = dot(low, g, ((1,), (0,)))
            grad_key = dk if x == 0 else grad_key + dk
            grad_value = dv if x == 0 else grad_value + dv
        total[:, :HEAD] = grad_key
        total[:, HEAD:] = grad_value
        for i in range(count):

            @pl.when(p == i)
            def _(i=i):
                grads[i][:, cols] = total[...].astype(grads[i].dtype)

    res = call(
        body, (where, src, lengths), (count, 2),
        [pl.BlockSpec((N, 2, 1, 256, HEAD), lambda p, l, *_: (0, 0, p + first, 0, l))]
        + [whole((256, 512))] * count + [ANY] * (len(into) + len(wait)),
        [pl.BlockSpec((N, 2, 1, 256, HEAD), lambda p, l, *_: (0, 0, p + first, 0, l))]
        + [whole((256, 512))] * count,
        [jax.ShapeDtypeStruct((N, 2, 2, 256, 256), BF)]
        + [
            jax.ShapeDtypeStruct((256, 512), BF if m else F32)
            for m in order
        ],
        "attend", (count * 6_000_000_000, (4 << 20) * count),
        [pltpu.VMEM((256, 256), BF), pltpu.VMEM((256, 256), F32)],
        {4 + count: 0} if into else {},
    )(where, src, lengths, moved, *kvs, *into, *wait)
    return res[0], res[1:]


def add_up(own, others, after):
    def body(a, b, c, d, *rest):
        rest[-1][...] = (a[...] + (b[...].astype(F32) + c[...] + d[...])).astype(BF)

    return small(
        body, (), [own, *others], after, jax.ShapeDtypeStruct((256, 512), BF), "add_up"
    )


def rows_to_send(where, came):
    def body(w, *refs):
        for n in range(N):
            for k in range(N):
                refs[N + n][k] = refs[k][minus(w[3], n)]

    return small(
        body, (where,), came, (), [jax.ShapeDtypeStruct((N, 2, 128, 128), BF)] * N,
        "rows_to_send",
    )


def weight_gradient(where, pieces, grads):
    def body(w, t0, t1, t2, t3, d, out):
        n = pl.program_id(0)
        for i, t in enumerate((t0, t1, t2, t3)):

            @pl.when(n == i)
            def _(t=t, i=i):
                for e in range(2):
                    part = None
                    for k in range(N):
                        p = dot(t[k, e], d[minus(w[2], k), 0, e], ((0,), (0,)))
                        part = p if part is None else part + p
                    if i == 0:
                        out[e] = part
                    else:
                        out[e] += part

    return call(
        body, (where,), (N,),
        [whole((N, 2, 128, 128))] * N
        + [pl.BlockSpec((N, 1, 2, 128, 512), lambda n, w: (0, lax.rem(w[3] + n, N), 0, 0, 0))],
        whole((2, 128, 512)), jax.ShapeDtypeStruct((2, 128, 512), F32), "weight_gradient",
        (2 * 256 * 2048 * 512, 6 << 20),
    )(where, *pieces, grads.reshape(N, N, 2, 128, 512))


def place(where, parts):
    rows = 64

    def body(w, *refs):
        outs = refs[-2:]
        slots = [(part, at) for part in refs[:2] for at in range(2)]
        for m, (part, at) in zip(ORDER, slots):
            for x in range(N):
                col = pl.multiple_of((x * N + minus(w[1], m)) * 256, 256)
                for a in range(2):
                    outs[a][:, pl.ds(col, 256)] = part[x, a, at]

    return call(
        body, (where,), (256 // rows,),
        [pl.BlockSpec((N, 2, 2, rows, 256), lambda i, w: (0, 0, 0, i, 0))] * 2,
        [pl.BlockSpec((rows, 4096), lambda i, w: (i, 0))] * 2,
        [jax.ShapeDtypeStruct((256, 4096), BF)] * 2, "place", (0, 8 << 20),
    )(where, *parts)


def per_device(text, src, lengths, kv_weight, queries, grad_out):
    group = lax.axis_index("dp")
    ctx = lax.axis_index("ctx")
    where = jnp.stack([ctx // N, ctx % N, group // N, group % N]).astype(jnp.int32)
    lengths = lengths.reshape(32)
    text, q, g = text[0], queries[0], grad_out[0]

    weight = lax.all_gather(jnp.swapaxes(kv_weight, 0, 1), "dp", axis=0)
    near = [text] + [r_shift(text, N - n) for n in (1, 2, 3)]
    packed = pack(ORDER[:2], where, q, g, [tiny(a) for a in near[1:]])
    moved = [exchange_x(packed)]
    packed = pack(ORDER[2:], where, q, g, [tiny(packed)])
    sends = text_to_send(where, src, near)
    picked = text_that_came(
        where, src, [sends[0]] + [y_shift(sends[k], k) for k in (1, 2, 3)]
    )
    along_z = jnp.stack([picked] + [z_shift(picked, n) for n in (1, 2, 3)])
    pieces = [along_z] + [x_shift(along_z, k) for k in (1, 2, 3)]

    kv, rows = project(where, pieces, weight)
    packed, kv = lax.optimization_barrier((packed, kv))
    moved.append(exchange_x(packed))
    kvs = [kv] + [z_shift(kv, m) for m in ORDER[1:]]
    rows = [rows[0]] + [y_shift(rows[k], k) for k in (1, 2, 3)]
    by_r = rows_to_send(where, rows)
    own_rows = [by_r[0]] + [r_shift(by_r[n], N - n) for n in (1, 2, 3)]
    waits = ([], [kvs[2], *rows[1:]], [], own_rows[1:])

    outs, grads, done = [None, None], [], 0
    for which, first, count in PARTS:
        part = slice(done, done + count)
        into = [outs[which]] if first else []
        wait = [tiny(a) for a in waits[done]]
        outs[which], d = attend(
            ORDER[part], first, where, src, lengths, moved[which], kvs[part], into, wait
        )
        for m, a in zip(ORDER[part], d):
            grads.append(z_shift(a, N - m) if m else a)
        done += count

    outs = [exchange_x(a) for a in outs]
    total = add_up(grads[0], grads[1:], [tiny(outs[0])])
    every_grad = lax.all_gather(total.reshape(2, 128, 512), "dp", axis=0)
    grad_weight = weight_gradient(where, own_rows, every_grad)
    attended, grad_queries = place(where, outs)
    return (attended[None], grad_queries[None], jnp.swapaxes(grad_weight, 0, 1))


def solution(mesh):
    placed = (
        P("dp", None, None, "ctx"),
        P(),
        P(),
        P("dp", None, "ctx"),
        P("dp", "ctx", None),
        P("dp", "ctx", None),
    )
    return jax.shard_map(
        per_device,
        mesh=mesh,
        in_specs=placed,
        out_specs=(P("dp", "ctx", None), P("dp", "ctx", None), P("dp", None, "ctx")),
        check_vma=False,
    )
```

```python
import math

import jax
import jax.numpy as jnp
from jax import lax
from jax.experimental import pallas as pl
from jax.experimental.pallas import tpu as pltpu
from jax.sharding import PartitionSpec as P

HEAD = 128
N = 4
ALONG_X = [[4 * x + z for x in range(N)] for z in range(N)]
BF = jnp.bfloat16
F32 = jnp.float32
PARAMS = pltpu.CompilerParams(vmem_limit_bytes=60 << 20)
ANY = pl.BlockSpec(memory_space=pl.ANY)
ORDER = (0, 1, 3, 2)
PARTS = ((0, 0), (0, 1), (1, 0), (1, 1))


def x_shift(a, k):
    return lax.ppermute(
        a, "ctx", [(4 * x + z, 4 * ((x + k) % N) + z) for x in range(N) for z in range(N)]
    )


def z_shift(a, m):
    return lax.ppermute(
        a, "ctx", [(4 * x + z, 4 * x + (z + m) % N) for x in range(N) for z in range(N)]
    )


def y_shift(a, k):
    return lax.ppermute(a, "dp", [(i, (i // N + k) % N * N + i % N) for i in range(16)])


def r_shift(a, n):
    return lax.ppermute(a, "dp", [(i, i // N * N + (i % N + n) % N) for i in range(16)])


def exchange_x(a):
    return lax.all_to_all(
        a, "ctx", split_axis=0, concat_axis=0, tiled=True, axis_index_groups=ALONG_X
    )


def dot(a, b, dims):
    return lax.dot_general(a, b, (dims, ((), ())), preferred_element_type=F32)


def minus(a, b):
    return lax.rem(a + N - b, N)


def whole(shape):
    return pl.BlockSpec(shape, lambda *_: (0,) * len(shape))


def call(body, scalars, grid, in_specs, out_specs, out_shape, name, cost, scratch=(), alias=(), params=PARAMS):
    return pl.pallas_call(
        body,
        grid_spec=pltpu.PrefetchScalarGridSpec(
            num_scalar_prefetch=len(scalars),
            grid=grid,
            in_specs=in_specs,
            out_specs=out_specs,
            scratch_shapes=list(scratch),
        ),
        out_shape=out_shape,
        input_output_aliases=dict(alias),
        cost_estimate=pl.CostEstimate(flops=cost[0], bytes_accessed=cost[1], transcendentals=0),
        compiler_params=params,
        name=name,
    )


def small(body, scalars, arrays, after, out_shape, name, cost=1 << 19):
    here = pl.BlockSpec(memory_space=pltpu.VMEM)
    return pl.pallas_call(
        body,
        in_specs=[pl.BlockSpec(memory_space=pltpu.SMEM)] * len(scalars)
        + [here] * len(arrays) + [ANY] * len(after),
        out_specs=jax.tree.map(lambda _: here, out_shape),
        out_shape=out_shape,
        cost_estimate=pl.CostEstimate(flops=0, bytes_accessed=cost, transcendentals=0),
        compiler_params=pltpu.CompilerParams(vmem_limit_bytes=16 << 20),
        name=name,
    )(*scalars, *arrays, *after)


def text_to_send(where, src, near):
    def body(w, src, *refs):
        for k in range(N):
            sample = src[lax.rem(w[2] + k, N) * N + w[3]]
            at = minus(lax.rem(sample, N), w[3])
            for n in range(N):

                @pl.when(at == n)
                def _(n=n, k=k):
                    refs[N + k][...] = refs[n][...]

    one = jax.ShapeDtypeStruct((2, 128, 128), BF)
    return small(body, (where, src), near, (), [one] * N, "text_to_send")


def text_that_came(where, src, came, after):
    def body(w, src, *refs):
        out = refs[-1]
        at = minus(w[2], src[w[2] * N + w[3]] // N)
        for k in range(N):

            @pl.when(at == k)
            def _(k=k):
                out[...] = refs[k][...]

    one = jax.ShapeDtypeStruct((2, 128, 128), BF)
    return small(body, (where, src), came, after, one, "text_that_came")


def tiny(a):
    return a[(0,) * (a.ndim - 2)][:16, :128]


def pack(order, where, queries, grad_out, after):
    rows = 64

    def body(w, q, g, *rest):
        out = rest[-1]
        for x in range(N):
            for i, m in enumerate(order):
                col = pl.multiple_of((x * N + minus(w[1], m)) * 256, 256)
                out[x, 0, i] = q[:, pl.ds(col, 256)]
                out[x, 1, i] = g[:, pl.ds(col, 256)]

    return call(
        body, (where,), (256 // rows,),
        [pl.BlockSpec((rows, 4096), lambda i, w: (i, 0))] * 2 + [ANY] * len(after),
        pl.BlockSpec((N, 2, len(order), rows, 256), lambda i, w: (0, 0, 0, i, 0)),
        jax.ShapeDtypeStruct((N, 2, len(order), 256, 256), BF), "pack", (0, 18 << 20),
    )(where, queries, grad_out, *after)


def project(where, pieces, weight):
    def body(w, t0, t1, t2, t3, wt, kv, *rest):
        rows, acc = rest[:N], rest[N]
        k = pl.program_id(0)
        for i, t in enumerate((t0, t1, t2, t3)):

            @pl.when(k == i)
            def _(t=t, i=i):
                for e in range(2):
                    part = None
                    for n in range(N):
                        d = dot(t[n, e], wt[0, minus(w[1], n), e], ((1,), (0,)))
                        part = d if part is None else part + d
                    if i == 0:
                        acc[e] = part
                    elif i < N - 1:
                        acc[e] += part
                    else:
                        kv[e] = (acc[e] + part).astype(BF)
                for j in range(N):

                    @pl.when(minus(minus(w[0], i), w[2]) == j)
                    def _():
                        for n in range(N):
                            rows[j][minus(w[1], n)] = t[n]

    def at(k, w):
        return (minus(w[0], k), 0, 0, 0, 0)

    quarter = (N, 2, 128, 128)
    kv, *rows = call(
        body, (where,), (N,),
        [whole(quarter)] * N + [pl.BlockSpec((1, N, 2, 128, 512), at)],
        [whole((2, 128, 512))] + [whole(quarter)] * N,
        [jax.ShapeDtypeStruct((2, 128, 512), BF)] + [jax.ShapeDtypeStruct(quarter, BF)] * N,
        "project", (2 * 256 * 2048 * 512, 6 << 20), [pltpu.VMEM((2, 128, 512), F32)],
        params=pltpu.CompilerParams(vmem_limit_bytes=16 << 20),
    )(where, *pieces, weight.reshape(N, N, 2, 128, 512))
    return kv.reshape(256, 512), rows


def attend(m, piece, where, src, lengths, moved, kv, into, wait):
    scale = 1.0 / math.sqrt(HEAD)

    def body(w, src, lengths, sent, kv, *refs):
        out, grads = refs[-2:]
        sample = src[w[2] * N + w[3]]
        row = lax.broadcasted_iota(jnp.int32, (256, 256), 0)
        valid = row < jnp.where(row < 128, lengths[2 * sample], lengths[2 * sample + 1] + 128)
        key, value = kv[:, :HEAD], kv[:, HEAD:]
        grad_key = grad_value = None
        for x in range(N):
            q, g = sent[x, 0, 0], sent[x, 1, 0]
            scores = dot(key, q, ((1,), (1,))) * scale
            scores = jnp.where(valid, scores, -1e30)
            weights = jnp.exp(scores - jnp.max(scores, axis=0, keepdims=True))
            probs = weights * (1.0 / jnp.sum(weights, axis=0, keepdims=True))
            low = probs.astype(BF)
            out[x, 0, 0] = dot(low, value, ((0,), (0,))).astype(BF)
            grad_probs = dot(value, g, ((1,), (1,)))
            delta = jnp.sum(probs * grad_probs, axis=0, keepdims=True)
            grad_scores = (probs * (grad_probs - delta) * scale).astype(BF)
            out[x, 1, 0] = dot(grad_scores, key, ((0,), (0,))).astype(BF)
            dk = dot(grad_scores, q, ((1,), (0,)))
            dv = dot(low, g, ((1,), (0,)))
            grad_key = dk if x == 0 else grad_key + dk
            grad_value = dv if x == 0 else grad_value + dv
        grads[:, :HEAD] = grad_key.astype(grads.dtype)
        grads[:, HEAD:] = grad_value.astype(grads.dtype)

    by_head = pl.BlockSpec((N, 2, 1, 256, HEAD), lambda l, *_: (0, 0, piece, 0, l))
    columns = pl.BlockSpec((256, 256), lambda l, *_: (0, l))
    return call(
        body, (where, src, lengths), (2,),
        [by_head, columns] + [ANY] * (len(into) + len(wait)),
        [by_head, columns],
        [
            jax.ShapeDtypeStruct((N, 2, 2, 256, 256), BF),
            jax.ShapeDtypeStruct((256, 512), BF if m else F32),
        ],
        "attend", (6_000_000_000, 4 << 20), (), {5: 0} if into else {},
    )(where, src, lengths, moved, kv, *into, *wait)


def add_first(own, others):
    def body(a, b, c, out):
        out[...] = a[...] + (b[...].astype(F32) + c[...])

    return small(
        body, (), [own, *others], (), jax.ShapeDtypeStruct((256, 512), F32), "add_first",
        16 << 20,
    )


def add_last(most, last, after):
    def body(a, b, *rest):
        rest[-1][...] = (a[...] + b[...]).astype(BF)

    return small(
        body, (), [most, last], after, jax.ShapeDtypeStruct((256, 512), BF), "add_last"
    )


def rows_to_send(where, came):
    def body(w, *refs):
        for n in range(N):
            for k in range(N):
                for e in range(2):
                    refs[N + n][k, e] = refs[k][minus(w[3], n), e].T

    return small(
        body, (where,), came, (), [jax.ShapeDtypeStruct((N, 2, 128, 128), BF)] * N,
        "rows_to_send",
    )


def weight_gradient(where, pieces, grads):
    def body(w, t0, t1, t2, t3, d, out, acc):
        n = pl.program_id(0)
        for i, t in enumerate((t0, t1, t2, t3)):

            @pl.when(n == i)
            def _(t=t, i=i):
                for e in range(2):
                    part = None
                    for k in range(N):
                        p = dot(t[k, e], d[minus(w[2], k), 0, e], ((1,), (0,)))
                        part = p if part is None else part + p
                    if i == 0:
                        acc[e] = part
                    elif i < N - 1:
                        acc[e] += part
                    else:
                        out[:, e, :] = acc[e] + part

    return call(
        body, (where,), (N,),
        [whole((N, 2, 128, 128))] * N
        + [pl.BlockSpec((N, 1, 2, 128, 512), lambda n, w: (0, lax.rem(w[3] + n, N), 0, 0, 0))],
        whole((128, 2, 512)), jax.ShapeDtypeStruct((128, 2, 512), F32), "weight_gradient",
        (2 * 256 * 2048 * 512, 6 << 20), [pltpu.VMEM((2, 128, 512), F32)],
    )(where, *pieces, grads.reshape(N, N, 2, 128, 512))


def place(where, parts):
    rows = 64

    def body(w, *refs):
        outs = refs[-2:]
        slots = [(part, at) for part in refs[:2] for at in range(2)]
        for m, (part, at) in zip(ORDER, slots):
            for x in range(N):
                col = pl.multiple_of((x * N + minus(w[1], m)) * 256, 256)
                for a in range(2):
                    outs[a][:, pl.ds(col, 256)] = part[x, a, at]

    return call(
        body, (where,), (256 // rows,),
        [pl.BlockSpec((N, 2, 2, rows, 256), lambda i, w: (0, 0, 0, i, 0))] * 2,
        [pl.BlockSpec((rows, 4096), lambda i, w: (i, 0))] * 2,
        [jax.ShapeDtypeStruct((256, 4096), BF)] * 2, "place", (0, 8 << 20),
    )(where, *parts)


def per_device(text, src, lengths, kv_weight, queries, grad_out):
    group = lax.axis_index("dp")
    ctx = lax.axis_index("ctx")
    where = jnp.stack([ctx // N, ctx % N, group // N, group % N]).astype(jnp.int32)
    lengths = lengths.reshape(32)
    text, q, g = text[0], queries[0], grad_out[0]

    weight = lax.all_gather(jnp.swapaxes(kv_weight, 0, 1), "dp", axis=0)
    near = [text] + [r_shift(text, N - n) for n in (1, 2, 3)]
    sends = text_to_send(where, src, near)
    packed = pack(ORDER[:2], where, q, g, [tiny(sends[0])])
    moved = [exchange_x(packed)]
    picked = text_that_came(
        where, src, [sends[0]] + [y_shift(sends[k], k) for k in (1, 2, 3)], [tiny(packed)]
    )
    packed = pack(ORDER[2:], where, q, g, [tiny(packed)])
    along_z = jnp.stack([picked] + [z_shift(picked, n) for n in (1, 2, 3)])
    pieces = [along_z] + [x_shift(along_z, k) for k in (1, 2, 3)]

    packed, *pieces = lax.optimization_barrier((packed, *pieces))
    moved.append(exchange_x(packed))
    kv, rows = project(where, pieces, weight)
    kvs = [kv] + [z_shift(kv, m) for m in ORDER[1:]]

    rows = [rows[0]] + [y_shift(rows[k], k) for k in (1, 2, 3)]
    by_r = rows_to_send(where, rows)
    own_rows = [by_r[0]] + [r_shift(by_r[n], N - n) for n in (1, 2, 3)]

    outs, grads = [None, None], []
    for i, (which, first) in enumerate(PARTS):
        into = [outs[which]] if first else []
        wait = ([], [kvs[2], *rows[1:]], [], own_rows[1:])[i]
        outs[which], d = attend(
            ORDER[i], first, where, src, lengths, moved[which], kvs[i], into,
            [tiny(a) for a in wait],
        )
        grads.append(z_shift(d, N - ORDER[i]) if i else d)

    outs = [exchange_x(a) for a in outs]
    after = [tiny(a) for a in [outs[0]]]
    total = add_last(add_first(grads[0], grads[1:3]), grads[3], after)
    every_grad = lax.all_gather(total.reshape(2, 128, 512), "dp", axis=0)
    grad_weight = weight_gradient(where, own_rows, every_grad)
    attended, grad_queries = place(where, outs)
    return (attended[None], grad_queries[None], grad_weight)


def solution(mesh):
    placed = (
        P("dp", None, None, "ctx"),
        P(),
        P(),
        P("dp", None, "ctx"),
        P("dp", "ctx", None),
        P("dp", "ctx", None),
    )
    return jax.shard_map(
        per_device,
        mesh=mesh,
        in_specs=placed,
        out_specs=(P("dp", "ctx", None), P("dp", "ctx", None), P("dp", None, "ctx")),
        check_vma=False,
    )
```

```python
import math

import jax
import jax.numpy as jnp
from jax import lax
from jax.experimental import pallas as pl
from jax.experimental.pallas import tpu as pltpu
from jax.sharding import PartitionSpec as P

HEAD = 128
N = 4
ALONG_X = [[4 * x + z for x in range(N)] for z in range(N)]
BF = jnp.bfloat16
F32 = jnp.float32
PARAMS = pltpu.CompilerParams(vmem_limit_bytes=60 << 20)
ANY = pl.BlockSpec(memory_space=pl.ANY)
ORDER = (0, 1, 3, 2)
PARTS = ((0, 0, 0, 0), (0, 1, 0, 1), (0, 2, 1, 0), (1, 0, 1, 1))


def x_shift(a, k):
    return lax.ppermute(
        a, "ctx", [(4 * x + z, 4 * ((x + k) % N) + z) for x in range(N) for z in range(N)]
    )


def z_shift(a, m):
    return lax.ppermute(
        a, "ctx", [(4 * x + z, 4 * x + (z + m) % N) for x in range(N) for z in range(N)]
    )


def y_shift(a, k):
    return lax.ppermute(a, "dp", [(i, (i // N + k) % N * N + i % N) for i in range(16)])


def r_shift(a, n):
    return lax.ppermute(a, "dp", [(i, i // N * N + (i % N + n) % N) for i in range(16)])


def exchange_x(a):
    return lax.all_to_all(
        a, "ctx", split_axis=0, concat_axis=0, tiled=True, axis_index_groups=ALONG_X
    )


def dot(a, b, dims):
    return lax.dot_general(a, b, (dims, ((), ())), preferred_element_type=F32)


def minus(a, b):
    return lax.rem(a + N - b, N)


def whole(shape):
    return pl.BlockSpec(shape, lambda *_: (0,) * len(shape))


def call(body, scalars, grid, in_specs, out_specs, out_shape, name, cost, scratch=(), alias=(), params=PARAMS):
    return pl.pallas_call(
        body,
        grid_spec=pltpu.PrefetchScalarGridSpec(
            num_scalar_prefetch=len(scalars),
            grid=grid,
            in_specs=in_specs,
            out_specs=out_specs,
            scratch_shapes=list(scratch),
        ),
        out_shape=out_shape,
        input_output_aliases=dict(alias),
        cost_estimate=pl.CostEstimate(flops=cost[0], bytes_accessed=cost[1], transcendentals=0),
        compiler_params=params,
        name=name,
    )


def small(body, scalars, arrays, after, out_shape, name, cost=1 << 19):
    here = pl.BlockSpec(memory_space=pltpu.VMEM)
    return pl.pallas_call(
        body,
        in_specs=[pl.BlockSpec(memory_space=pltpu.SMEM)] * len(scalars)
        + [here] * len(arrays) + [ANY] * len(after),
        out_specs=jax.tree.map(lambda _: here, out_shape),
        out_shape=out_shape,
        cost_estimate=pl.CostEstimate(flops=0, bytes_accessed=cost, transcendentals=0),
        compiler_params=pltpu.CompilerParams(vmem_limit_bytes=16 << 20),
        name=name,
    )(*scalars, *arrays, *after)


def text_to_send(where, src, near):
    def body(w, src, *refs):
        for k in range(N):
            sample = src[lax.rem(w[2] + k, N) * N + w[3]]
            at = minus(lax.rem(sample, N), w[3])
            for n in range(N):

                @pl.when(at == n)
                def _(n=n, k=k):
                    refs[N + k][...] = refs[n][...]

    one = jax.ShapeDtypeStruct((2, 128, 128), BF)
    return small(body, (where, src), near, (), [one] * N, "text_to_send")


def text_that_came(where, src, came, after):
    def body(w, src, *refs):
        out = refs[-1]
        at = minus(w[2], src[w[2] * N + w[3]] // N)
        for k in range(N):

            @pl.when(at == k)
            def _(k=k):
                out[...] = refs[k][...]

    one = jax.ShapeDtypeStruct((2, 128, 128), BF)
    return small(body, (where, src), came, after, one, "text_that_came")


def tiny(a):
    return a[(0,) * (a.ndim - 2)][:16, :128]


def pack(order, where, queries, grad_out, after):
    rows = 64

    def body(w, q, g, *rest):
        out = rest[-1]
        for x in range(N):
            for i, m in enumerate(order):
                col = pl.multiple_of((x * N + minus(w[1], m)) * 256, 256)
                out[x, 0, i] = q[:, pl.ds(col, 256)]
                out[x, 1, i] = g[:, pl.ds(col, 256)]

    return call(
        body, (where,), (256 // rows,),
        [pl.BlockSpec((rows, 4096), lambda i, w: (i, 0))] * 2 + [ANY] * len(after),
        pl.BlockSpec((N, 2, len(order), rows, 256), lambda i, w: (0, 0, 0, i, 0)),
        jax.ShapeDtypeStruct((N, 2, len(order), 256, 256), BF), "pack", (0, 18 << 20),
    )(where, queries, grad_out, *after)


def project(where, pieces, weight):
    def body(w, t0, t1, t2, t3, wt, kv, *rest):
        rows, acc = rest[:N], rest[N]
        k = pl.program_id(0)
        for i, t in enumerate((t0, t1, t2, t3)):

            @pl.when(k == i)
            def _(t=t, i=i):
                for e in range(2):
                    part = None
                    for n in range(N):
                        d = dot(t[n, e], wt[0, minus(w[1], n), e], ((1,), (0,)))
                        part = d if part is None else part + d
                    if i == 0:
                        acc[e] = part
                    elif i < N - 1:
                        acc[e] += part
                    else:
                        kv[e] = (acc[e] + part).astype(BF)
                for j in range(N):

                    @pl.when(minus(minus(w[0], i), w[2]) == j)
                    def _():
                        for n in range(N):
                            rows[j][minus(w[1], n)] = t[n]

    def at(k, w):
        return (minus(w[0], k), 0, 0, 0, 0)

    quarter = (N, 2, 128, 128)
    kv, *rows = call(
        body, (where,), (N,),
        [whole(quarter)] * N + [pl.BlockSpec((1, N, 2, 128, 512), at)],
        [whole((2, 128, 512))] + [whole(quarter)] * N,
        [jax.ShapeDtypeStruct((2, 128, 512), BF)] + [jax.ShapeDtypeStruct(quarter, BF)] * N,
        "project", (2 * 256 * 2048 * 512, 6 << 20), [pltpu.VMEM((2, 128, 512), F32)],
        params=pltpu.CompilerParams(vmem_limit_bytes=16 << 20),
    )(where, *pieces, weight.reshape(N, N, 2, 128, 512))
    return kv.reshape(256, 512), rows


def attend(m, piece, slot, where, src, lengths, moved, kv, into, wait):
    scale = 1.0 / math.sqrt(HEAD)

    def body(w, src, lengths, sent, kv, *refs):
        out, grads = refs[-2:]
        sample = src[w[2] * N + w[3]]
        row = lax.broadcasted_iota(jnp.int32, (256, 256), 0)
        valid = row < jnp.where(row < 128, lengths[2 * sample], lengths[2 * sample + 1] + 128)
        key, value = kv[:, :HEAD], kv[:, HEAD:]
        grad_key = grad_value = None
        for x in range(N):
            q, g = sent[x, 0, 0], sent[x, 1, 0]
            scores = dot(key, q, ((1,), (1,))) * scale
            scores = jnp.where(valid, scores, -1e30)
            weights = jnp.exp(scores - jnp.max(scores, axis=0, keepdims=True))
            probs = weights * (1.0 / jnp.sum(weights, axis=0, keepdims=True))
            low = probs.astype(BF)
            out[x, 0, 0] = dot(low, value, ((0,), (0,))).astype(BF)
            grad_probs = dot(value, g, ((1,), (1,)))
            delta = jnp.sum(probs * grad_probs, axis=0, keepdims=True)
            grad_scores = (probs * (grad_probs - delta) * scale).astype(BF)
            out[x, 1, 0] = dot(grad_scores, key, ((0,), (0,))).astype(BF)
            dk = dot(grad_scores, q, ((1,), (0,)))
            dv = dot(low, g, ((1,), (0,)))
            grad_key = dk if x == 0 else grad_key + dk
            grad_value = dv if x == 0 else grad_value + dv
        grads[:, :HEAD] = grad_key.astype(grads.dtype)
        grads[:, HEAD:] = grad_value.astype(grads.dtype)

    def by_head(at):
        return pl.BlockSpec((N, 2, 1, 256, HEAD), lambda l, *_: (0, 0, at, 0, l))

    columns = pl.BlockSpec((256, 256), lambda l, *_: (0, l))
    return call(
        body, (where, src, lengths), (2,),
        [by_head(piece), columns] + [ANY] * (len(into) + len(wait)),
        [by_head(slot), columns],
        [
            jax.ShapeDtypeStruct((N, 2, 2, 256, 256), BF),
            jax.ShapeDtypeStruct((256, 512), BF if m else F32),
        ],
        "attend", (6_000_000_000, 4 << 20), (), {5: 0} if into else {},
    )(where, src, lengths, moved, kv, *into, *wait)


def add_first(own, others):
    def body(a, b, c, out):
        out[...] = a[...] + (b[...].astype(F32) + c[...])

    return small(
        body, (), [own, *others], (), jax.ShapeDtypeStruct((256, 512), F32), "add_first",
        16 << 20,
    )


def add_last(most, last, after):
    def body(a, b, *rest):
        rest[-1][...] = (a[...] + b[...]).astype(BF)

    return small(
        body, (), [most, last], after, jax.ShapeDtypeStruct((256, 512), BF), "add_last"
    )


def relay(a, after):
    def body(a, *rest):
        rest[-1][...] = a[...]

    return small(body, (), [a], after, jax.ShapeDtypeStruct(a.shape, a.dtype), "relay")


def rows_to_send(where, came):
    def body(w, *refs):
        for n in range(N):
            for k in range(N):
                for e in range(2):
                    refs[N + n][k, e] = refs[k][minus(w[3], n), e].T

    return small(
        body, (where,), came, (), [jax.ShapeDtypeStruct((N, 2, 128, 128), BF)] * N,
        "rows_to_send",
    )


def weight_gradient(where, pieces, grads):
    def body(w, t0, t1, t2, t3, d, out, acc):
        n = pl.program_id(0)
        for i, t in enumerate((t0, t1, t2, t3)):

            @pl.when(n == i)
            def _(t=t, i=i):
                for e in range(2):
                    part = None
                    for k in range(N):
                        p = dot(t[k, e], d[minus(w[2], k), 0, e], ((1,), (0,)))
                        part = p if part is None else part + p
                    if i == 0:
                        acc[e] = part
                    elif i < N - 1:
                        acc[e] += part
                    else:
                        out[:, e, :] = acc[e] + part

    return call(
        body, (where,), (N,),
        [whole((N, 2, 128, 128))] * N
        + [pl.BlockSpec((N, 1, 2, 128, 512), lambda n, w: (0, lax.rem(w[3] + n, N), 0, 0, 0))],
        whole((128, 2, 512)), jax.ShapeDtypeStruct((128, 2, 512), F32), "weight_gradient",
        (2 * 256 * 2048 * 512, 6 << 20), [pltpu.VMEM((2, 128, 512), F32)],
    )(where, *pieces, grads.reshape(N, N, 2, 128, 512))


def place(where, parts):
    rows = 64

    def body(w, *refs):
        outs = refs[-2:]
        slots = [(part, at) for part in refs[:2] for at in range(2)]
        for m, (part, at) in zip(ORDER, slots):
            for x in range(N):
                col = pl.multiple_of((x * N + minus(w[1], m)) * 256, 256)
                for a in range(2):
                    outs[a][:, pl.ds(col, 256)] = part[x, a, at]

    return call(
        body, (where,), (256 // rows,),
        [pl.BlockSpec((N, 2, 2, rows, 256), lambda i, w: (0, 0, 0, i, 0))] * 2,
        [pl.BlockSpec((rows, 4096), lambda i, w: (i, 0))] * 2,
        [jax.ShapeDtypeStruct((256, 4096), BF)] * 2, "place", (0, 8 << 20),
    )(where, *parts)


def per_device(text, src, lengths, kv_weight, queries, grad_out):
    group = lax.axis_index("dp")
    ctx = lax.axis_index("ctx")
    where = jnp.stack([ctx // N, ctx % N, group // N, group % N]).astype(jnp.int32)
    lengths = lengths.reshape(32)
    text, q, g = text[0], queries[0], grad_out[0]

    weight = lax.all_gather(jnp.swapaxes(kv_weight, 0, 1), "dp", axis=0)
    near = [text] + [r_shift(text, N - n) for n in (1, 2, 3)]
    sends = text_to_send(where, src, near)
    packed = pack(ORDER[:3], where, q, g, [tiny(sends[0])])
    moved = [exchange_x(packed)]
    picked = text_that_came(
        where, src, [sends[0]] + [y_shift(sends[k], k) for k in (1, 2, 3)], [tiny(packed)]
    )
    packed = pack(ORDER[3:], where, q, g, [tiny(packed)])
    along_z = jnp.stack([picked] + [z_shift(picked, n) for n in (1, 2, 3)])
    pieces = [along_z] + [x_shift(along_z, k) for k in (1, 2, 3)]

    packed, *pieces = lax.optimization_barrier((packed, *pieces))
    moved.append(exchange_x(packed))
    kv, rows = project(where, pieces, weight)
    kvs = [kv] + [z_shift(kv, m) for m in ORDER[1:3]]

    rows = [rows[0]] + [y_shift(rows[k], k) for k in (1, 2, 3)]
    by_r = rows_to_send(where, rows)
    own_rows = [by_r[0]] + [r_shift(by_r[n], N - n) for n in (1, 2, 3)]

    outs, grads = [None, None], []
    for i, (came, piece, which, slot) in enumerate(PARTS):
        into = [outs[which]] if slot else []
        wait = ([], [kvs[2], *rows[1:]], [], own_rows[1:])[i]
        outs[which], d = attend(
            ORDER[i], piece, slot, where, src, lengths, moved[came], kvs[i], into,
            [tiny(a) for a in wait],
        )
        grads.append(z_shift(d, N - ORDER[i]) if i else d)
        if i == 0:
            kvs.append(z_shift(relay(kv, [tiny(d)]), ORDER[3]))

    outs = [exchange_x(a) for a in outs]
    after = [tiny(a) for a in [outs[0]]]
    total = add_last(add_first(grads[0], grads[1:3]), grads[3], after)
    every_grad = lax.all_gather(total.reshape(2, 128, 512), "dp", axis=0)
    grad_weight = weight_gradient(where, own_rows, every_grad)
    attended, grad_queries = place(where, outs)
    return (attended[None], grad_queries[None], grad_weight)


def solution(mesh):
    placed = (
        P("dp", None, None, "ctx"),
        P(),
        P(),
        P("dp", None, "ctx"),
        P("dp", "ctx", None),
        P("dp", "ctx", None),
    )
    return jax.shard_map(
        per_device,
        mesh=mesh,
        in_specs=placed,
        out_specs=(P("dp", "ctx", None), P("dp", "ctx", None), P("dp", None, "ctx")),
        check_vma=False,
    )
```
